32 devices in a mesh: dp: 4 (over y, x), vocab: 8 (over z, core).
Axes of the slice: x: 2, y: 2, z: 4, core: 2. Of those that a mesh axis runs over, the one named last changes fastest.
Arguments:
- query_hidden: bfloat16 [8, 128, 4096], P('dp', None, 'vocab'), may hold values from -144 to 144
- passage_hidden: bfloat16 [8, 256, 4096], P('dp', None, 'vocab'), may hold values from -144 to 144
- head_weight: bfloat16 [4096, 16384], P(None, 'vocab'), may hold values from -6 to 6
- query_mask: int32 [8, 128], P('dp'), may hold values from 0 to 1, as said below
- passage_mask: int32 [8, 256], P('dp'), may hold values from 0 to 1, as said below
- positive: int32 [8], replicated, may hold values from 0 to 7
Outputs:
- grad_query_hidden: bfloat16 [8, 128, 4096], P('dp', None, 'vocab')
- grad_passage_hidden: bfloat16 [8, 256, 4096], P('dp', None, 'vocab')
- query_loss: float32 [8], P('dp')
The draws below stay inside these ranges and needn't reach their ends.
Inputs may be any that keep to these rules, and one draw needn't show every extreme that they name: `query_mask`: the live tokens of each query are a prefix of 32 to 128 positions. `passage_mask`: the live tokens of each passage are a prefix of 64 to 256 positions.
All inputs are finite; a program needn't handle non-finite values.
Results may differ from the reference program's by a relative error of at most 0.0095.
Values may be sent and summed in bfloat16 or wider, within the bound.
A program may use at most 128 MiB of HBM per device.

```python
import math
import jax
import jax.numpy as jnp
from jax import lax

D = 4096
QLEN = 128
PLEN = 256
VOCAB = 16384
QUERIES = 8
PASSAGES = 8


def hidden_states(key, count, length):
    values = jnp.clip(jax.random.normal(key, (count, length, D), jnp.float32), -6.0, 6.0)
    return values.astype(jnp.bfloat16)


def prefix_mask(key, count, length):
    lengths = jax.random.randint(key, (count,), length // 4, length + 1)
    return (jnp.arange(length, dtype=jnp.int32)[None, :] < lengths[:, None]).astype(jnp.int32)


def draw_query_hidden(key, part):
    return hidden_states(jax.random.fold_in(key, 11), QUERIES, QLEN)


def draw_passage_hidden(key, part):
    return hidden_states(jax.random.fold_in(key, 13), PASSAGES, PLEN)


def draw_head_weight(key, part):
    inner = jax.random.fold_in(key, 23)
    column = jnp.arange(VOCAB, dtype=jnp.float32) / (VOCAB - 1.0)
    values = jnp.clip(jax.random.normal(inner, (D, VOCAB), jnp.float32), -6.0, 6.0)
    ramp = jnp.exp(math.log(0.4) + math.log(10.0) * column)
    return (values * ramp[None, :] / math.sqrt(D)).astype(jnp.bfloat16)


def draw_query_mask(key, part):
    return prefix_mask(jax.random.fold_in(key, 17), QUERIES, QLEN)


def draw_passage_mask(key, part):
    return prefix_mask(jax.random.fold_in(key, 19), PASSAGES, PLEN)


def with_ends(array, rng, least, largest):
    index_at = [jax.random.randint(jax.random.fold_in(rng, axis), (), 0, length) for axis, length in enumerate(array.shape)]
    longest = array.shape.index(max(array.shape))
    neighbour = index_at[:longest] + [(index_at[longest] + 1) % array.shape[longest]] + index_at[longest + 1:]
    return array.at[tuple(index_at)].set(least).at[tuple(neighbour)].set(largest)


def setup_inputs(seed: int = 0) -> dict:
    arg_keys = jax.random.split(jax.random.key(seed), 7)
    return {
        "query_hidden": draw_query_hidden(jax.random.fold_in(arg_keys[6], 71), 0),
        "passage_hidden": draw_passage_hidden(jax.random.fold_in(arg_keys[6], 71), 0),
        "head_weight": draw_head_weight(jax.random.fold_in(arg_keys[6], 71), 0),
        "query_mask": draw_query_mask(jax.random.fold_in(arg_keys[6], 71), 0),
        "passage_mask": draw_passage_mask(jax.random.fold_in(arg_keys[6], 71), 0),
        "positive": with_ends(jax.random.randint(arg_keys[5], (QUERIES,), 0, PASSAGES), jax.random.fold_in(arg_keys[5], 1), 0, PASSAGES - 1).astype(jnp.int32),
    }


normalizer_sharpness = 0.2
score_div = 16.0
loss_scale = 65536.0


def pool_seq(lexicon_projection_lines, live):
    divided_similarity_matrix = lexicon_projection_lines / normalizer_sharpness
    live_rows = live[:, None] > 0
    largest_element = jnp.max(jnp.where(live_rows, divided_similarity_matrix, -1e30), axis=0)
    expo = jnp.where(live_rows, jnp.exp(divided_similarity_matrix - largest_element[None, :]), 0.0)
    cumulative_accumulator = jnp.sum(expo, axis=0)
    softened_rectifier_output = normalizer_sharpness * (largest_element + jnp.log(cumulative_accumulator))
    return softened_rectifier_output, expo / cumulative_accumulator[None, :]


def forward_pool(hidden, mask, head_weight):
    def single(args):
        rows, live = args
        lexicon_projection_lines = jnp.dot(rows, head_weight, preferred_element_type=jnp.float32)
        softened_rectifier_output, share = pool_seq(lexicon_projection_lines, live)
        return softened_rectifier_output
    return lax.map(single, (hidden, mask))


def reverse_max_reduce(hidden, mask, head_weight, dpooled):
    def single(args):
        rows, live, dpool = args
        lexicon_projection_lines = jnp.dot(rows, head_weight, preferred_element_type=jnp.float32)
        softened_rectifier_output, share = pool_seq(lexicon_projection_lines, live)
        dsmooth = dpool * jnp.where(softened_rectifier_output > 0, 1.0 / (1.0 + jnp.maximum(softened_rectifier_output, 0.0)), 0.0)
        dlogits = (share * dsmooth[None, :]).astype(jnp.bfloat16)
        return jnp.dot(dlogits, head_weight.T, preferred_element_type=jnp.float32).astype(jnp.bfloat16)
    return lax.map(single, (hidden, mask, dpooled))


def reference(query_hidden, passage_hidden, head_weight, query_mask, passage_mask, positive):
    q_smooth = forward_pool(query_hidden, query_mask, head_weight)
    p_smooth = forward_pool(passage_hidden, passage_mask, head_weight)
    q_pooled = jnp.log1p(jnp.maximum(q_smooth, 0.0))
    p_pooled = jnp.log1p(jnp.maximum(p_smooth, 0.0))
    scores = jnp.dot(q_pooled, p_pooled.T, precision=lax.Precision.HIGHEST, preferred_element_type=jnp.float32) / score_div
    largest_element = jnp.max(scores, axis=1)
    lse = largest_element + jnp.log(jnp.sum(jnp.exp(scores - largest_element[:, None]), axis=1))
    picked = (positive[:, None] == jnp.arange(PASSAGES, dtype=jnp.int32)[None, :]).astype(jnp.float32)
    query_loss = lse - jnp.sum(scores * picked, axis=1)
    probs = jnp.exp(scores - lse[:, None])
    dscores = (probs - picked) * (loss_scale / QUERIES)
    dq_pooled = jnp.dot(dscores, p_pooled, precision=lax.Precision.HIGHEST, preferred_element_type=jnp.float32) / score_div
    grad_passage_summary = jnp.dot(dscores.T, q_pooled, precision=lax.Precision.HIGHEST, preferred_element_type=jnp.float32) / score_div
    grad_query_hidden = reverse_max_reduce(query_hidden, query_mask, head_weight, dq_pooled)
    grad_passage_hidden = reverse_max_reduce(passage_hidden, passage_mask, head_weight, grad_passage_summary)
    return grad_query_hidden, grad_passage_hidden, query_loss
```

```python
import functools

import jax
import jax.numpy as jnp
from jax import lax
from jax.experimental import pallas as pl
from jax.experimental.pallas import tpu as pltpu
from jax.sharding import PartitionSpec as P

sharpness = 0.2
score_div = 16.0
loss_scale = 65536.0
lanes = 128
low = -1e30
MESH = pl.DeviceIdType.MESH


def nt_dot(left, right):
    return lax.dot_general(
        left, right, (((1,), (1,)), ((), ())), preferred_element_type=jnp.float32
    )


def kernel(
    cfg,
    q_hbm, p_hbm, w_hbm, q_mask, p_mask, picked_ref,
    gq_ref, gp_ref, loss_ref,
    w, xg, acc, dl, in_l, in_r, out_l, out_r, sib_in, sib_out, own, part,
    smooth, total, coef, pooled, scores, dscores, losses,
    load_sem, w_sem, recv1, send1, recv_p, send_p, recv_s, send_s,
    recv_l, recv_r, send_l, send_r, recv_sib, send_sib,
):
    G, V, B, R, F, C, q_count, p_count, q_len = cfg
    L = V // 2
    passages = G * p_count
    g = lax.axis_index("dp")
    me = lax.axis_index("vocab")
    c = lax.rem(me, 2)
    i = lax.div(me, 2)
    sib = me + 1 - 2 * c
    has_left, has_right = i > 0, i < L - 1

    loads = []
    for b in range(B):
        src = q_hbm if b == 0 else p_hbm.at[pl.ds((b - 1) * R, R)]
        loads.append(pltpu.make_async_copy(src, xg.at[me, b], load_sem.at[b]))
    for load in loads:
        load.start()
    w_load = pltpu.make_async_copy(w_hbm, w, w_sem)
    w_load.start()

    barrier = pltpu.get_barrier_semaphore()
    for k in range(1, V):
        pl.semaphore_signal(
            barrier, inc=1, device_id={"vocab": lax.rem(me + k, V)}, device_id_type=MESH
        )
    for k in range(1, G):
        pl.semaphore_signal(
            barrier, inc=1, device_id={"dp": lax.rem(g + k, G)}, device_id_type=MESH
        )
    pl.semaphore_wait(barrier, V - 1 + G - 1)
    for load in loads:
        load.wait()

    def hop(v, b, way, target):
        return pltpu.make_async_remote_copy(
            src_ref=xg.at[v, b],
            dst_ref=xg.at[v, b],
            send_sem=send1.at[way, v, b],
            recv_sem=recv1.at[v, b],
            device_id={"vocab": target},
            device_id_type=MESH,
        )

    def send_own(b):
        @pl.when(has_right)
        def _():
            hop(me, b, 0, me + 2).start()

        @pl.when(has_left)
        def _():
            hop(me, b, 1, me - 2).start()

        hop(me, b, 2, sib).start()

    send_own(0)
    acc[...] = jnp.zeros_like(acc)
    pooled[g] = jnp.zeros(pooled.shape[1:], jnp.float32)
    w_load.wait()

    tile = min(512, C)

    def mm1(v, b):
        def body(n, carry):
            cols = pl.ds(pl.multiple_of(n * tile, tile), tile)
            rows = pl.ds(pl.multiple_of(v * F, F), F)
            acc[b, :, cols] += jnp.dot(
                xg[v, b], w[rows, cols], preferred_element_type=jnp.float32
            )
            return carry

        lax.fori_loop(0, C // tile, body, 0)

    ptile = min(256, C)

    def pool(b):
        if b == 0:
            seqs = [(k, k * q_len, q_len, q_mask, k) for k in range(q_count)]
        else:
            seqs = [(q_count + b - 1, 0, R, p_mask, b - 1)]
        for row, first, length, mask, at in seqs:
            live_len = jnp.sum(
                mask[pl.ds(at, 1), :].astype(jnp.float32), axis=1, keepdims=True
            )

            def body(n, carry, row=row, first=first, length=length, live_len=live_len):
                cols = pl.ds(pl.multiple_of(n * ptile, ptile), ptile)
                place = lax.broadcasted_iota(jnp.int32, (length, ptile), 0)
                live = place.astype(jnp.float32) < live_len
                x = jnp.where(live, acc[b, pl.ds(first, length), cols] * (1.0 / sharpness), low)
                top = jnp.max(x, axis=0, keepdims=True)
                e = jnp.where(live, jnp.exp(x - top), 0.0)
                acc[b, pl.ds(first, length), cols] = e
                s = jnp.sum(e, axis=0, keepdims=True)
                sm = sharpness * (top + jnp.log(s))
                smooth[row, :, cols] = sm
                total[row, :, cols] = s
                pooled[g, pl.ds(row, 1), cols] = jnp.log1p(jnp.maximum(sm, 0.0))
                return carry

            lax.fori_loop(0, C // ptile, body, 0)

    def gather_step(s, carry):
        b, h = lax.div(s, L), lax.rem(s, L)
        main = s < B * L
        left, right = i - h, i + h
        from_left = jnp.logical_and(main, left >= 0)
        from_right = jnp.logical_and(main, jnp.logical_and(right < L, h > 0))

        @pl.when(jnp.logical_and(h == 0, b + 1 < B))
        def _():
            send_own(b + 1)

        @pl.when(jnp.logical_and(from_left, h > 0))
        def _():
            v = 2 * left + c
            hop(v, b, 0, sib).wait_recv()

            @pl.when(has_right)
            def _():
                hop(v, b, 0, me + 2).start()

            hop(v, b, 2, sib).start()

        @pl.when(from_right)
        def _():
            v = 2 * right + c
            hop(v, b, 1, sib).wait_recv()

            @pl.when(has_left)
            def _():
                hop(v, b, 1, me - 2).start()

            hop(v, b, 2, sib).start()

        @pl.when(from_left)
        def _():
            mm1(2 * left + c, b)

        @pl.when(from_right)
        def _():
            mm1(2 * right + c, b)

        t = jnp.maximum(s - 1, 0)
        b1, h1 = lax.div(t, L), lax.rem(t, L)
        left1, right1 = i - h1, i + h1

        @pl.when(jnp.logical_and(s > 0, left1 >= 0))
        def _():
            v = 2 * left1 + 1 - c
            hop(v, b1, 2, sib).wait_recv()
            mm1(v, b1)

        @pl.when(jnp.logical_and(s > 0, jnp.logical_and(right1 < L, h1 > 0)))
        def _():
            v = 2 * right1 + 1 - c
            hop(v, b1, 2, sib).wait_recv()
            mm1(v, b1)

        for done in range(B):
            @pl.when(s == (done + 1) * L)
            def _(done=done):
                pool(done)

        return carry

    lax.fori_loop(0, B * L + 1, gather_step, 0)

    def pooled_copy(group, k):
        return pltpu.make_async_remote_copy(
            src_ref=pooled.at[group],
            dst_ref=pooled.at[group],
            send_sem=send_p.at[k],
            recv_sem=recv_p.at[group],
            device_id={"dp": lax.rem(g + k, G)},
            device_id_type=MESH,
        )

    for k in range(1, G):
        pooled_copy(g, k).start()
    for k in range(1, G):
        pooled_copy(lax.rem(g + k, G), k).wait_recv()

    lane = lax.broadcasted_iota(jnp.int32, (8, lanes), 1)
    blocks = [jnp.zeros((8, lanes), jnp.float32) for _ in range(G)]
    for p in range(passages):
        row = q_count + p % p_count
        vector = pooled[p // p_count, row : row + 1, :]
        for k in range(G):
            value = jnp.sum(pooled[k] * vector, axis=1, keepdims=True)
            blocks[k] = jnp.where(lane == p, value, blocks[k])
    for k in range(G):
        scores[me, k] = blocks[k]

    def score_copy(v, k):
        return pltpu.make_async_remote_copy(
            src_ref=scores.at[v],
            dst_ref=scores.at[v],
            send_sem=send_s.at[k],
            recv_sem=recv_s.at[v],
            device_id={"vocab": lax.rem(me + k, V)},
            device_id_type=MESH,
        )

    for k in range(1, V):
        score_copy(me, k).start()
    for k in range(1, V):
        score_copy(lax.rem(me + k, V), k).wait_recv()

    row_at = lax.broadcasted_iota(jnp.int32, (8, lanes), 0)
    valid = jnp.logical_and(lane < passages, row_at < q_count)
    for k in range(G):
        sc = scores[0, k]
        for v in range(1, V):
            sc = sc + scores[v, k]
        sc = sc / score_div
        masked = jnp.where(lane < passages, sc, low)
        top = jnp.max(masked, axis=1, keepdims=True)
        lse = top + jnp.log(
            jnp.sum(jnp.where(lane < passages, jnp.exp(masked - top), 0.0), axis=1, keepdims=True)
        )
        hot = picked_ref[k]
        losses[k] = lse - jnp.sum(jnp.where(lane < passages, sc, 0.0) * hot, axis=1, keepdims=True) + jnp.zeros_like(sc)
        dscores[k] = jnp.where(
            valid, (jnp.exp(masked - lse) - hot) * (loss_scale / (G * q_count)), 0.0
        )
    loss_ref[...] = losses[g]

    mine = dscores[g]
    dq = jnp.zeros((8, C), jnp.float32)
    for p in range(passages):
        row = q_count + p % p_count
        dq = dq + mine[:, p : p + 1] * pooled[p // p_count, row : row + 1, :]

    def factor(row, dpool):
        sm = smooth[row]
        gate = jnp.where(sm > 0, 1.0 / (1.0 + jnp.maximum(sm, 0.0)), 0.0)
        coef[row] = dpool * (1.0 / score_div) * gate / total[row]

    for k in range(q_count):
        factor(k, dq[k : k + 1, :])
    for k in range(p_count):
        dp = jnp.zeros((8, C), jnp.float32)
        for group in range(G):
            column = jnp.sum(
                jnp.where(lane == g * p_count + k, dscores[group], 0.0), axis=1, keepdims=True
            )
            dp = dp + column * pooled[group]
        factor(q_count + k, jnp.sum(dp, axis=0, keepdims=True))

    def make_dl(b):
        if b == 0:
            seqs = [(k, k * q_len, q_len) for k in range(q_count)]
        else:
            seqs = [(q_count + b - 1, 0, R)]
        for row, first, length in seqs:
            def body(n, carry, row=row, first=first, length=length):
                cols = pl.ds(pl.multiple_of(n * ptile, ptile), ptile)
                dl[b, pl.ds(first, length), cols] = (
                    acc[b, pl.ds(first, length), cols] * coef[row, :, cols]
                ).astype(jnp.bfloat16)
                return carry

            lax.fori_loop(0, C // ptile, body, 0)

    ftile = min(256, F)

    def mm2(v, b, store):
        def body(n, carry):
            at = pl.multiple_of(n * ftile, ftile)
            rows = pl.ds(pl.multiple_of(v * F + at, ftile), ftile)
            store(pl.ds(at, ftile), nt_dot(dl[b], w[rows, :]))
            return carry

        lax.fori_loop(0, F // ftile, body, 0)

    def sib_copy(b, j):
        return pltpu.make_async_remote_copy(
            src_ref=sib_out.at[b, j], dst_ref=sib_in.at[b, j],
            send_sem=send_sib.at[b, j], recv_sem=recv_sib.at[b, j],
            device_id={"vocab": sib}, device_id_type=MESH,
        )

    def right_copy(b, d):
        return pltpu.make_async_remote_copy(
            src_ref=out_r.at[b, d], dst_ref=in_l.at[b, d],
            send_sem=send_r.at[b, d], recv_sem=recv_l.at[b, d],
            device_id={"vocab": me + 2}, device_id_type=MESH,
        )

    def left_copy(b, d):
        return pltpu.make_async_remote_copy(
            src_ref=out_l.at[b, d], dst_ref=in_r.at[b, d],
            send_sem=send_l.at[b, d], recv_sem=recv_r.at[b, d],
            device_id={"vocab": me - 2}, device_id_type=MESH,
        )

    def for_sibling(j, b):
        def store(cols, value):
            sib_out[b, j, :, cols] = value.astype(jnp.bfloat16)

        mm2(2 * j + 1 - c, b, store)
        sib_copy(b, j).start()

    def for_me(j, b, way):
        def store(cols, value):
            part[way, :, cols] = value

        mm2(2 * j + c, b, store)

    def scatter_step(s, carry):
        b, d = lax.div(s, L), L - 1 - lax.rem(s, L)
        for block in range(B):
            @pl.when(s == block * L)
            def _(block=block):
                make_dl(block)

        right, left = i + d, i - d
        go_right = right < L
        go_left = jnp.logical_and(left >= 0, d > 0)

        @pl.when(go_right)
        def _():
            for_sibling(right, b)

        @pl.when(go_left)
        def _():
            for_sibling(left, b)

        @pl.when(jnp.logical_and(go_right, d > 0))
        def _():
            for_me(right, b, 0)

        @pl.when(go_left)
        def _():
            for_me(left, b, 1)

        @pl.when(d == 0)
        def _():
            def store(cols, value):
                own[b, :, cols] = value

            mm2(me, b, store)

        @pl.when(jnp.logical_and(go_right, d > 0))
        def _():
            sib_copy(b, right).wait_recv()
            part[0] += sib_in[b, right].astype(jnp.float32)

            @pl.when(has_left)
            def _():
                right_copy(b, d).wait_recv()
                part[0] += in_l[b, d].astype(jnp.float32)

            out_r[b, d - 1] = part[0].astype(jnp.bfloat16)
            right_copy(b, d - 1).start()

        @pl.when(go_left)
        def _():
            sib_copy(b, left).wait_recv()
            part[1] += sib_in[b, left].astype(jnp.float32)

            @pl.when(has_right)
            def _():
                left_copy(b, d).wait_recv()
                part[1] += in_r[b, d].astype(jnp.float32)

            out_l[b, d - 1] = part[1].astype(jnp.bfloat16)
            left_copy(b, d - 1).start()

        return carry

    lax.fori_loop(0, B * L, scatter_step, 0)

    for b in range(B):
        sib_copy(b, i).wait_recv()
        own[b] += sib_in[b, i].astype(jnp.float32)

        @pl.when(has_left)
        def _():
            right_copy(b, 0).wait_recv()
            own[b] += in_l[b, 0].astype(jnp.float32)

        @pl.when(has_right)
        def _():
            left_copy(b, 0).wait_recv()
            own[b] += in_r[b, 0].astype(jnp.float32)

        if b == 0:
            gq_ref[...] = own[b].astype(jnp.bfloat16)
        else:
            gp_ref[pl.ds((b - 1) * R, R), :] = own[b].astype(jnp.bfloat16)

    for k in range(1, G):
        pooled_copy(g, k).wait_send()
    for k in range(1, V):
        score_copy(me, k).wait_send()

    def drain(s, carry):
        b, j = lax.div(s, L), lax.rem(s, L)
        v = 2 * j + c
        hop(v, b, 2, sib).wait_send()
        sib_copy(b, j).wait_send()

        @pl.when(jnp.logical_and(has_right, j <= i))
        def _():
            hop(v, b, 0, me + 2).wait_send()

        @pl.when(jnp.logical_and(has_left, j >= i))
        def _():
            hop(v, b, 1, me - 2).wait_send()

        @pl.when(jnp.logical_and(j > 0, i + j < L))
        def _():
            right_copy(b, j - 1).wait_send()

        @pl.when(jnp.logical_and(j > 0, i - j >= 0))
        def _():
            left_copy(b, j - 1).wait_send()

        return carry

    lax.fori_loop(0, B * L, drain, 0)


def on_device(G, V, query_hidden, passage_hidden, head_weight, query_mask, passage_mask, positive):
    q_count, q_len, F = query_hidden.shape
    p_count, p_len, _ = passage_hidden.shape
    D, C = head_weight.shape
    R = p_len
    assert q_count * q_len == R and q_count + p_count <= 8
    B = 1 + p_count
    L = V // 2
    hot = positive[:, None] == jnp.arange(lanes, dtype=jnp.int32)[None, :]
    picked = jnp.pad(
        hot.astype(jnp.float32).reshape(G, q_count, lanes), ((0, 0), (0, 8 - q_count), (0, 0))
    )
    cfg = (G, V, B, R, F, C, q_count, p_count, q_len)
    seqs = q_count + p_count
    bf, f32, dma = jnp.bfloat16, jnp.float32, pltpu.SemaphoreType.DMA
    vmem, anywhere = pl.BlockSpec(memory_space=pltpu.VMEM), pl.BlockSpec(memory_space=pl.ANY)
    line = pltpu.VMEM((B, L - 1, R, F), bf)
    gq, gp, loss = pl.pallas_call(
        functools.partial(kernel, cfg),
        out_shape=(
            jax.ShapeDtypeStruct((R, F), bf),
            jax.ShapeDtypeStruct((p_count * R, F), bf),
            jax.ShapeDtypeStruct((8, lanes), f32),
        ),
        in_specs=[anywhere, anywhere, anywhere, vmem, vmem, vmem],
        out_specs=(vmem, vmem, vmem),
        scratch_shapes=[
            pltpu.VMEM((D, C), bf),
            pltpu.VMEM((V, B, R, F), bf),
            pltpu.VMEM((B, R, C), f32),
            pltpu.VMEM((B, R, C), bf),
            line, line, line, line,
            pltpu.VMEM((B, L, R, F), bf),
            pltpu.VMEM((B, L, R, F), bf),
            pltpu.VMEM((B, R, F), f32),
            pltpu.VMEM((2, R, F), f32),
            pltpu.VMEM((seqs, 1, C), f32),
            pltpu.VMEM((seqs, 1, C), f32),
            pltpu.VMEM((seqs, 1, C), f32),
            pltpu.VMEM((G, 8, C), f32),
            pltpu.VMEM((V, G, 8, lanes), f32),
            pltpu.VMEM((G, 8, lanes), f32),
            pltpu.VMEM((G, 8, lanes), f32),
            dma((B,)),
            dma,
            dma((V, B)),
            dma((3, V, B)),
            dma((G,)),
            dma((G,)),
            dma((V,)),
            dma((V,)),
            dma((B, L - 1)),
            dma((B, L - 1)),
            dma((B, L - 1)),
            dma((B, L - 1)),
            dma((B, L)),
            dma((B, L)),
        ],
        compiler_params=pltpu.CompilerParams(
            collective_id=0, has_side_effects=True, vmem_limit_bytes=60 * 1024 * 1024
        ),
    )(
        query_hidden.reshape(R, F),
        passage_hidden.reshape(p_count * R, F),
        head_weight,
        query_mask,
        passage_mask,
        picked,
    )
    return (
        gq.reshape(query_hidden.shape),
        gp.reshape(passage_hidden.shape),
        loss[:q_count, 0],
    )


def solution(mesh):
    return jax.shard_map(
        functools.partial(on_device, mesh.shape["dp"], mesh.shape["vocab"]),
        mesh=mesh,
        in_specs=(
            P("dp", None, "vocab"),
            P("dp", None, "vocab"),
            P(None, "vocab"),
            P("dp", None),
            P("dp", None),
            P(),
        ),
        out_specs=(P("dp", None, "vocab"), P("dp", None, "vocab"), P("dp")),
        check_vma=False,
    )
```

```python
import functools

import jax
import jax.numpy as jnp
from jax import lax
from jax.experimental import pallas as pl
from jax.experimental.pallas import tpu as pltpu
from jax.sharding import PartitionSpec as P

sharpness = 0.2
score_div = 16.0
loss_scale = 65536.0
lanes = 128
low = -1e30
MESH = pl.DeviceIdType.MESH


def nt_dot(left, right):
    return lax.dot_general(
        left, right, (((1,), (1,)), ((), ())), preferred_element_type=jnp.float32
    )


def kernel(
    cfg,
    q_hbm, p_hbm, w_hbm, q_mask, p_mask, picked_ref,
    out_ref, loss_ref,
    w, xg, acc, dl, in_l, in_r, out_l, out_r, sib_in, sib_out, part,
    smooth, total, coef, pooled, scores, dscores, losses,
    load_sem, w_sem, recv1, send1, recv_p, send_p, recv_s, send_s,
    recv_l, recv_r, send_l, send_r, recv_sib, send_sib,
):
    G, V, B, R, F, C, q_count, p_count, q_len = cfg
    L = V // 2
    passages = G * p_count
    g = lax.axis_index("dp")
    me = lax.axis_index("vocab")
    c = lax.rem(me, 2)
    i = lax.div(me, 2)
    sib = me + 1 - 2 * c
    has_left, has_right = i > 0, i < L - 1

    loads = []
    for b in range(B):
        src = q_hbm if b == 0 else p_hbm.at[pl.ds((b - 1) * R, R)]
        loads.append(pltpu.make_async_copy(src, xg.at[me, b], load_sem.at[b]))
    for load in loads:
        load.start()
    w_load = pltpu.make_async_copy(w_hbm, w, w_sem)
    w_load.start()

    barrier = pltpu.get_barrier_semaphore()
    for k in range(1, V):
        pl.semaphore_signal(
            barrier, inc=1, device_id={"vocab": lax.rem(me + k, V)}, device_id_type=MESH
        )
    for k in range(1, G):
        pl.semaphore_signal(
            barrier, inc=1, device_id={"dp": lax.rem(g + k, G)}, device_id_type=MESH
        )
    pl.semaphore_wait(barrier, V - 1 + G - 1)
    for load in loads:
        load.wait()

    def hop(v, b, way, target):
        return pltpu.make_async_remote_copy(
            src_ref=xg.at[v, b],
            dst_ref=xg.at[v, b],
            send_sem=send1.at[way, v, b],
            recv_sem=recv1.at[v, b],
            device_id={"vocab": target},
            device_id_type=MESH,
        )

    def send_own(b):
        @pl.when(has_right)
        def _():
            hop(me, b, 0, me + 2).start()

        @pl.when(has_left)
        def _():
            hop(me, b, 1, me - 2).start()

        hop(me, b, 2, sib).start()

    send_own(0)
    acc[...] = jnp.zeros_like(acc)
    pooled[g] = jnp.zeros(pooled.shape[1:], jnp.float32)
    w_load.wait()

    tile = min(512, C)

    def mm1(v, b):
        def body(n, carry):
            cols = pl.ds(pl.multiple_of(n * tile, tile), tile)
            rows = pl.ds(pl.multiple_of(v * F, F), F)
            acc[b, :, cols] += jnp.dot(
                xg[v, b], w[rows, cols], preferred_element_type=jnp.float32
            )
            return carry

        lax.fori_loop(0, C // tile, body, 0)

    ptile = min(256, C)

    def pool(b):
        if b == 0:
            seqs = [(k, k * q_len, q_len, q_mask, k) for k in range(q_count)]
        else:
            seqs = [(q_count + b - 1, 0, R, p_mask, b - 1)]
        for row, first, length, mask, at in seqs:
            live_len = jnp.sum(
                mask[pl.ds(at, 1), :].astype(jnp.float32), axis=1, keepdims=True
            )

            def body(n, carry, row=row, first=first, length=length, live_len=live_len):
                cols = pl.ds(pl.multiple_of(n * ptile, ptile), ptile)
                place = lax.broadcasted_iota(jnp.int32, (length, ptile), 0)
                live = place.astype(jnp.float32) < live_len
                x = jnp.where(live, acc[b, pl.ds(first, length), cols] * (1.0 / sharpness), low)
                top = jnp.max(x, axis=0, keepdims=True)
                e = jnp.where(live, jnp.exp(x - top), 0.0)
                acc[b, pl.ds(first, length), cols] = e
                s = jnp.sum(e, axis=0, keepdims=True)
                sm = sharpness * (top + jnp.log(s))
                smooth[row, :, cols] = sm
                total[row, :, cols] = s
                pooled[g, pl.ds(row, 1), cols] = jnp.log1p(jnp.maximum(sm, 0.0))
                return carry

            lax.fori_loop(0, C // ptile, body, 0)

    def gather_step(s, carry):
        b, h = lax.div(s, L), lax.rem(s, L)
        main = s < B * L
        left, right = i - h, i + h
        from_left = jnp.logical_and(main, left >= 0)
        from_right = jnp.logical_and(main, jnp.logical_and(right < L, h > 0))

        @pl.when(jnp.logical_and(h == 0, b + 1 < B))
        def _():
            send_own(b + 1)

        @pl.when(jnp.logical_and(from_left, h > 0))
        def _():
            v = 2 * left + c
            hop(v, b, 0, sib).wait_recv()

            @pl.when(has_right)
            def _():
                hop(v, b, 0, me + 2).start()

            hop(v, b, 2, sib).start()

        @pl.when(from_right)
        def _():
            v = 2 * right + c
            hop(v, b, 1, sib).wait_recv()

            @pl.when(has_left)
            def _():
                hop(v, b, 1, me - 2).start()

            hop(v, b, 2, sib).start()

        @pl.when(from_left)
        def _():
            mm1(2 * left + c, b)

        @pl.when(from_right)
        def _():
            mm1(2 * right + c, b)

        t = jnp.maximum(s - 1, 0)
        b1, h1 = lax.div(t, L), lax.rem(t, L)
        left1, right1 = i - h1, i + h1

        @pl.when(jnp.logical_and(s > 0, left1 >= 0))
        def _():
            v = 2 * left1 + 1 - c
            hop(v, b1, 2, sib).wait_recv()
            mm1(v, b1)

        @pl.when(jnp.logical_and(s > 0, jnp.logical_and(right1 < L, h1 > 0)))
        def _():
            v = 2 * right1 + 1 - c
            hop(v, b1, 2, sib).wait_recv()
            mm1(v, b1)

        for done in range(B):
            @pl.when(s == (done + 1) * L)
            def _(done=done):
                pool(done)

        return carry

    lax.fori_loop(0, B * L + 1, gather_step, 0)

    def pooled_copy(group, k):
        return pltpu.make_async_remote_copy(
            src_ref=pooled.at[group],
            dst_ref=pooled.at[group],
            send_sem=send_p.at[k],
            recv_sem=recv_p.at[group],
            device_id={"dp": lax.rem(g + k, G)},
            device_id_type=MESH,
        )

    for k in range(1, G):
        pooled_copy(g, k).start()
    for k in range(1, G):
        pooled_copy(lax.rem(g + k, G), k).wait_recv()

    lane = lax.broadcasted_iota(jnp.int32, (8, lanes), 1)
    blocks = [jnp.zeros((8, lanes), jnp.float32) for _ in range(G)]
    for p in range(passages):
        row = q_count + p % p_count
        vector = pooled[p // p_count, row : row + 1, :]
        for k in range(G):
            value = jnp.sum(pooled[k] * vector, axis=1, keepdims=True)
            blocks[k] = jnp.where(lane == p, value, blocks[k])
    for k in range(G):
        scores[me, k] = blocks[k]

    def score_copy(v, k):
        return pltpu.make_async_remote_copy(
            src_ref=scores.at[v],
            dst_ref=scores.at[v],
            send_sem=send_s.at[k],
            recv_sem=recv_s.at[v],
            device_id={"vocab": lax.rem(me + k, V)},
            device_id_type=MESH,
        )

    for k in range(1, V):
        score_copy(me, k).start()
    for k in range(1, V):
        score_copy(lax.rem(me + k, V), k).wait_recv()

    row_at = lax.broadcasted_iota(jnp.int32, (8, lanes), 0)
    valid = jnp.logical_and(lane < passages, row_at < q_count)
    for k in range(G):
        sc = scores[0, k]
        for v in range(1, V):
            sc = sc + scores[v, k]
        sc = sc / score_div
        masked = jnp.where(lane < passages, sc, low)
        top = jnp.max(masked, axis=1, keepdims=True)
        lse = top + jnp.log(
            jnp.sum(jnp.where(lane < passages, jnp.exp(masked - top), 0.0), axis=1, keepdims=True)
        )
        hot = picked_ref[k]
        losses[k] = lse - jnp.sum(jnp.where(lane < passages, sc, 0.0) * hot, axis=1, keepdims=True) + jnp.zeros_like(sc)
        dscores[k] = jnp.where(
            valid, (jnp.exp(masked - lse) - hot) * (loss_scale / (G * q_count)), 0.0
        )
    loss_ref[...] = losses[g]

    mine = dscores[g]
    dq = jnp.zeros((8, C), jnp.float32)
    for p in range(passages):
        row = q_count + p % p_count
        dq = dq + mine[:, p : p + 1] * pooled[p // p_count, row : row + 1, :]

    def factor(row, dpool):
        sm = smooth[row]
        gate = jnp.where(sm > 0, 1.0 / (1.0 + jnp.maximum(sm, 0.0)), 0.0)
        coef[row] = dpool * (1.0 / score_div) * gate / total[row]

    for k in range(q_count):
        factor(k, dq[k : k + 1, :])
    for k in range(p_count):
        dp = jnp.zeros((8, C), jnp.float32)
        for group in range(G):
            column = jnp.sum(
                jnp.where(lane == g * p_count + k, dscores[group], 0.0), axis=1, keepdims=True
            )
            dp = dp + column * pooled[group]
        factor(q_count + k, jnp.sum(dp, axis=0, keepdims=True))

    for b in range(B):
        if b == 0:
            seqs = [(k, k * q_len, q_len) for k in range(q_count)]
        else:
            seqs = [(q_count + b - 1, 0, R)]
        for row, first, length in seqs:
            def body(n, carry, b=b, row=row, first=first, length=length):
                cols = pl.ds(pl.multiple_of(n * ptile, ptile), ptile)
                dl[pl.ds(b * R + first, length), cols] = (
                    acc[b, pl.ds(first, length), cols] * coef[row, :, cols]
                ).astype(jnp.bfloat16)
                return carry

            lax.fori_loop(0, C // ptile, body, 0)

    ftile = min(256, F)

    def mm2(v, store):
        def body(n, carry):
            at = pl.multiple_of(n * ftile, ftile)
            rows = pl.ds(pl.multiple_of(v * F + at, ftile), ftile)
            store(pl.ds(at, ftile), nt_dot(dl[...], w[rows, :]))
            return carry

        lax.fori_loop(0, F // ftile, body, 0)

    def sib_copy(j):
        return pltpu.make_async_remote_copy(
            src_ref=sib_out.at[j], dst_ref=sib_in.at[j],
            send_sem=send_sib.at[j], recv_sem=recv_sib.at[j],
            device_id={"vocab": sib}, device_id_type=MESH,
        )

    def right_copy(b, d):
        return pltpu.make_async_remote_copy(
            src_ref=out_r.at[b, d], dst_ref=in_l.at[b, d],
            send_sem=send_r.at[b, d], recv_sem=recv_l.at[b, d],
            device_id={"vocab": me + 2}, device_id_type=MESH,
        )

    def left_copy(b, d):
        return pltpu.make_async_remote_copy(
            src_ref=out_l.at[b, d], dst_ref=in_r.at[b, d],
            send_sem=send_l.at[b, d], recv_sem=recv_r.at[b, d],
            device_id={"vocab": me - 2}, device_id_type=MESH,
        )

    def for_sibling(j):
        def store(cols, value):
            sib_out[j, :, cols] = value.astype(jnp.bfloat16)

        mm2(2 * j + 1 - c, store)
        sib_copy(j).start()

    def for_me(j, way):
        def store(cols, value):
            part[way, :, cols] = value

        mm2(2 * j + c, store)

    def pass_on(way, j, b, d, more, copy, arrived, out):
        rows = pl.ds(b * R, R)

        @pl.when(more)
        def _():
            copy(b, d).wait_recv()
            out[b, d - 1] = (
                part[way, rows]
                + sib_in[j, rows].astype(jnp.float32)
                + arrived[b, d].astype(jnp.float32)
            ).astype(jnp.bfloat16)

        @pl.when(jnp.logical_not(more))
        def _():
            out[b, d - 1] = (
                part[way, rows] + sib_in[j, rows].astype(jnp.float32)
            ).astype(jnp.bfloat16)

        copy(b, d - 1).start()

    def scatter_step(s, carry):
        d = L - 1 - s
        right, left = i + d, i - d
        go_right = right < L
        go_left = jnp.logical_and(left >= 0, d > 0)
        on_right = jnp.logical_and(go_right, d > 0)

        @pl.when(go_right)
        def _():
            for_sibling(right)

        @pl.when(go_left)
        def _():
            for_sibling(left)

        @pl.when(go_right)
        def _():
            for_me(right, 0)

        @pl.when(go_left)
        def _():
            for_me(left, 1)

        @pl.when(on_right)
        def _():
            sib_copy(right).wait_recv()

        @pl.when(go_left)
        def _():
            sib_copy(left).wait_recv()

        for b in range(B):
            @pl.when(on_right)
            def _(b=b):
                pass_on(0, right, b, d, has_left, right_copy, in_l, out_r)

            @pl.when(go_left)
            def _(b=b):
                pass_on(1, left, b, d, has_right, left_copy, in_r, out_l)

        return carry

    lax.fori_loop(0, L, scatter_step, 0)

    sib_copy(i).wait_recv()
    for b in range(B):
        rows = pl.ds(b * R, R)

        @pl.when(jnp.logical_and(has_left, has_right))
        def _():
            right_copy(b, 0).wait_recv()
            left_copy(b, 0).wait_recv()
            out_ref[rows, :] = (
                part[0, rows]
                + sib_in[i, rows].astype(jnp.float32)
                + in_l[b, 0].astype(jnp.float32)
                + in_r[b, 0].astype(jnp.float32)
            ).astype(jnp.bfloat16)

        @pl.when(jnp.logical_and(has_left, jnp.logical_not(has_right)))
        def _():
            right_copy(b, 0).wait_recv()
            out_ref[rows, :] = (
                part[0, rows]
                + sib_in[i, rows].astype(jnp.float32)
                + in_l[b, 0].astype(jnp.float32)
            ).astype(jnp.bfloat16)

        @pl.when(jnp.logical_and(jnp.logical_not(has_left), has_right))
        def _():
            left_copy(b, 0).wait_recv()
            out_ref[rows, :] = (
                part[0, rows]
                + sib_in[i, rows].astype(jnp.float32)
                + in_r[b, 0].astype(jnp.float32)
            ).astype(jnp.bfloat16)

        @pl.when(jnp.logical_not(jnp.logical_or(has_left, has_right)))
        def _():
            out_ref[rows, :] = (
                part[0, rows] + sib_in[i, rows].astype(jnp.float32)
            ).astype(jnp.bfloat16)

    for k in range(1, G):
        pooled_copy(g, k).wait_send()
    for k in range(1, V):
        score_copy(me, k).wait_send()

    def drain(s, carry):
        b, j = lax.div(s, L), lax.rem(s, L)
        v = 2 * j + c
        hop(v, b, 2, sib).wait_send()

        @pl.when(jnp.logical_and(has_right, j <= i))
        def _():
            hop(v, b, 0, me + 2).wait_send()

        @pl.when(jnp.logical_and(has_left, j >= i))
        def _():
            hop(v, b, 1, me - 2).wait_send()

        @pl.when(jnp.logical_and(j > 0, i + j < L))
        def _():
            right_copy(b, j - 1).wait_send()

        @pl.when(jnp.logical_and(j > 0, i - j >= 0))
        def _():
            left_copy(b, j - 1).wait_send()

        return carry

    lax.fori_loop(0, B * L, drain, 0)
    for j in range(L):
        sib_copy(j).wait_send()


def on_device(G, V, query_hidden, passage_hidden, head_weight, query_mask, passage_mask, positive):
    q_count, q_len, F = query_hidden.shape
    p_count, p_len, _ = passage_hidden.shape
    D, C = head_weight.shape
    R = p_len
    assert q_count * q_len == R and q_count + p_count <= 8
    B = 1 + p_count
    L = V // 2
    hot = positive[:, None] == jnp.arange(lanes, dtype=jnp.int32)[None, :]
    picked = jnp.pad(
        hot.astype(jnp.float32).reshape(G, q_count, lanes), ((0, 0), (0, 8 - q_count), (0, 0))
    )
    cfg = (G, V, B, R, F, C, q_count, p_count, q_len)
    seqs = q_count + p_count
    bf, f32, dma = jnp.bfloat16, jnp.float32, pltpu.SemaphoreType.DMA
    vmem, anywhere = pl.BlockSpec(memory_space=pltpu.VMEM), pl.BlockSpec(memory_space=pl.ANY)
    line = pltpu.VMEM((B, L - 1, R, F), bf)
    grads, loss = pl.pallas_call(
        functools.partial(kernel, cfg),
        out_shape=(
            jax.ShapeDtypeStruct((B * R, F), bf),
            jax.ShapeDtypeStruct((8, lanes), f32),
        ),
        in_specs=[anywhere, anywhere, anywhere, vmem, vmem, vmem],
        out_specs=(vmem, vmem),
        scratch_shapes=[
            pltpu.VMEM((D, C), bf),
            pltpu.VMEM((V, B, R, F), bf),
            pltpu.VMEM((B, R, C), f32),
            pltpu.VMEM((B * R, C), bf),
            line, line, line, line,
            pltpu.VMEM((L, B * R, F), bf),
            pltpu.VMEM((L, B * R, F), bf),
            pltpu.VMEM((2, B * R, F), f32),
            pltpu.VMEM((seqs, 1, C), f32),
            pltpu.VMEM((seqs, 1, C), f32),
            pltpu.VMEM((seqs, 1, C), f32),
            pltpu.VMEM((G, 8, C), f32),
            pltpu.VMEM((V, G, 8, lanes), f32),
            pltpu.VMEM((G, 8, lanes), f32),
            pltpu.VMEM((G, 8, lanes), f32),
            dma((B,)),
            dma,
            dma((V, B)),
            dma((3, V, B)),
            dma((G,)),
            dma((G,)),
            dma((V,)),
            dma((V,)),
            dma((B, L - 1)),
            dma((B, L - 1)),
            dma((B, L - 1)),
            dma((B, L - 1)),
            dma((L,)),
            dma((L,)),
        ],
        compiler_params=pltpu.CompilerParams(
            collective_id=0, has_side_effects=True, vmem_limit_bytes=60 * 1024 * 1024
        ),
    )(
        query_hidden.reshape(R, F),
        passage_hidden.reshape(p_count * R, F),
        head_weight,
        query_mask,
        passage_mask,
        picked,
    )
    return (
        grads[:R].reshape(query_hidden.shape),
        grads[R:].reshape(passage_hidden.shape),
        loss[:q_count, 0],
    )


def solution(mesh):
    return jax.shard_map(
        functools.partial(on_device, mesh.shape["dp"], mesh.shape["vocab"]),
        mesh=mesh,
        in_specs=(
            P("dp", None, "vocab"),
            P("dp", None, "vocab"),
            P(None, "vocab"),
            P("dp", None),
            P("dp", None),
            P(),
        ),
        out_specs=(P("dp", None, "vocab"), P("dp", None, "vocab"), P("dp")),
        check_vma=False,
    )
```

```python
import functools

import jax
import jax.numpy as jnp
from jax import lax
from jax.experimental import pallas as pl
from jax.experimental.pallas import tpu as pltpu
from jax.sharding import PartitionSpec as P

sharpness = 0.2
score_div = 16.0
loss_scale = 65536.0
lanes = 128
low = -1e30
MESH = pl.DeviceIdType.MESH


def nt_dot(left, right):
    return lax.dot_general(
        left, right, (((1,), (1,)), ((), ())), preferred_element_type=jnp.float32
    )


def kernel(
    cfg,
    q_hbm, p_hbm, w_hbm, q_mask, p_mask, picked_ref,
    out_ref, loss_ref,
    w, xg, acc, dl, in_l, in_r, out_l, out_r, sib_in, sib_out, part,
    smooth, total, coef, pooled, scores, dscores, losses,
    load_sem, w_sem, recv1, send1, recv_p, send_p, recv_s, send_s,
    recv_l, recv_r, send_l, send_r, recv_sib, send_sib,
):
    G, V, B, R, F, C, q_count, p_count, q_len = cfg
    L = V // 2
    passages = G * p_count
    g = lax.axis_index("dp")
    me = lax.axis_index("vocab")
    c = lax.rem(me, 2)
    i = lax.div(me, 2)
    sib = me + 1 - 2 * c
    has_left, has_right = i > 0, i < L - 1

    loads = []
    for b in range(B):
        src = q_hbm if b == 0 else p_hbm.at[pl.ds((b - 1) * R, R)]
        loads.append(pltpu.make_async_copy(src, xg.at[me, b], load_sem.at[b]))
    for load in loads:
        load.start()
    w_load = pltpu.make_async_copy(w_hbm, w, w_sem)
    w_load.start()

    barrier = pltpu.get_barrier_semaphore()
    for k in range(1, V):
        pl.semaphore_signal(
            barrier, inc=1, device_id={"vocab": lax.rem(me + k, V)}, device_id_type=MESH
        )
    for k in range(1, G):
        pl.semaphore_signal(
            barrier, inc=1, device_id={"dp": lax.rem(g + k, G)}, device_id_type=MESH
        )
    pl.semaphore_wait(barrier, V - 1 + G - 1)
    for load in loads:
        load.wait()

    def hop(v, b, way, target):
        return pltpu.make_async_remote_copy(
            src_ref=xg.at[v, b],
            dst_ref=xg.at[v, b],
            send_sem=send1.at[way, v, b],
            recv_sem=recv1.at[v, b],
            device_id={"vocab": target},
            device_id_type=MESH,
        )

    def send_own(b):
        @pl.when(has_right)
        def _():
            hop(me, b, 0, me + 2).start()

        @pl.when(has_left)
        def _():
            hop(me, b, 1, me - 2).start()

        hop(me, b, 2, sib).start()

    send_own(0)
    acc[...] = jnp.zeros_like(acc)
    pooled[g] = jnp.zeros(pooled.shape[1:], jnp.float32)
    w_load.wait()

    tile = min(512, C)

    def mm1(v, b):
        def body(n, carry):
            cols = pl.ds(pl.multiple_of(n * tile, tile), tile)
            rows = pl.ds(pl.multiple_of(v * F, F), F)
            acc[b, :, cols] += jnp.dot(
                xg[v, b], w[rows, cols], preferred_element_type=jnp.float32
            )
            return carry

        lax.fori_loop(0, C // tile, body, 0)

    ptile = min(256, C)

    def pool(b):
        if b == 0:
            seqs = [(k, k * q_len, q_len, q_mask, k) for k in range(q_count)]
        else:
            seqs = [(q_count + b - 1, 0, R, p_mask, b - 1)]
        for row, first, length, mask, at in seqs:
            live_len = jnp.sum(
                mask[pl.ds(at, 1), :].astype(jnp.float32), axis=1, keepdims=True
            )

            def body(n, carry, row=row, first=first, length=length, live_len=live_len):
                cols = pl.ds(pl.multiple_of(n * ptile, ptile), ptile)
                place = lax.broadcasted_iota(jnp.int32, (length, ptile), 0)
                live = place.astype(jnp.float32) < live_len
                x = jnp.where(live, acc[b, pl.ds(first, length), cols] * (1.0 / sharpness), low)
                top = jnp.max(x, axis=0, keepdims=True)
                e = jnp.where(live, jnp.exp(x - top), 0.0)
                acc[b, pl.ds(first, length), cols] = e
                s = jnp.sum(e, axis=0, keepdims=True)
                sm = sharpness * (top + jnp.log(s))
                smooth[row, :, cols] = sm
                total[row, :, cols] = s
                pooled[g, pl.ds(row, 1), cols] = jnp.log1p(jnp.maximum(sm, 0.0))
                return carry

            lax.fori_loop(0, C // ptile, body, 0)

    def gather_step(s, carry):
        b, h = lax.div(s, L), lax.rem(s, L)
        main = s < B * L
        left, right = i - h, i + h
        from_left = jnp.logical_and(main, left >= 0)
        from_right = jnp.logical_and(main, jnp.logical_and(right < L, h > 0))

        @pl.when(jnp.logical_and(h == 0, b + 1 < B))
        def _():
            send_own(b + 1)

        @pl.when(jnp.logical_and(from_left, h > 0))
        def _():
            v = 2 * left + c
            hop(v, b, 0, sib).wait_recv()

            @pl.when(has_right)
            def _():
                hop(v, b, 0, me + 2).start()

            hop(v, b, 2, sib).start()

        @pl.when(from_right)
        def _():
            v = 2 * right + c
            hop(v, b, 1, sib).wait_recv()

            @pl.when(has_left)
            def _():
                hop(v, b, 1, me - 2).start()

            hop(v, b, 2, sib).start()

        @pl.when(from_left)
        def _():
            mm1(2 * left + c, b)

        @pl.when(from_right)
        def _():
            mm1(2 * right + c, b)

        t = jnp.maximum(s - 1, 0)
        b1, h1 = lax.div(t, L), lax.rem(t, L)
        left1, right1 = i - h1, i + h1

        @pl.when(jnp.logical_and(s > 0, left1 >= 0))
        def _():
            v = 2 * left1 + 1 - c
            hop(v, b1, 2, sib).wait_recv()
            mm1(v, b1)

        @pl.when(jnp.logical_and(s > 0, jnp.logical_and(right1 < L, h1 > 0)))
        def _():
            v = 2 * right1 + 1 - c
            hop(v, b1, 2, sib).wait_recv()
            mm1(v, b1)

        for done in range(B):
            @pl.when(s == (done + 1) * L)
            def _(done=done):
                pool(done)

        return carry

    lax.fori_loop(0, B * L + 1, gather_step, 0)

    def pooled_copy(group, k):
        return pltpu.make_async_remote_copy(
            src_ref=pooled.at[group],
            dst_ref=pooled.at[group],
            send_sem=send_p.at[k],
            recv_sem=recv_p.at[group],
            device_id={"dp": lax.rem(g + k, G)},
            device_id_type=MESH,
        )

    for k in range(1, G):
        pooled_copy(g, k).start()
    for k in range(1, G):
        pooled_copy(lax.rem(g + k, G), k).wait_recv()

    lane = lax.broadcasted_iota(jnp.int32, (8, lanes), 1)
    blocks = [jnp.zeros((8, lanes), jnp.float32) for _ in range(G)]
    for p in range(passages):
        row = q_count + p % p_count
        vector = pooled[p // p_count, row : row + 1, :]
        for k in range(G):
            value = jnp.sum(pooled[k] * vector, axis=1, keepdims=True)
            blocks[k] = jnp.where(lane == p, value, blocks[k])
    for k in range(G):
        scores[me, k] = blocks[k]

    def score_copy(v, k):
        return pltpu.make_async_remote_copy(
            src_ref=scores.at[v],
            dst_ref=scores.at[v],
            send_sem=send_s.at[k],
            recv_sem=recv_s.at[v],
            device_id={"vocab": lax.rem(me + k, V)},
            device_id_type=MESH,
        )

    for k in range(1, V):
        score_copy(me, k).start()
    for k in range(1, V):
        score_copy(lax.rem(me + k, V), k).wait_recv()

    row_at = lax.broadcasted_iota(jnp.int32, (8, lanes), 0)
    valid = jnp.logical_and(lane < passages, row_at < q_count)
    for k in range(G):
        sc = scores[0, k]
        for v in range(1, V):
            sc = sc + scores[v, k]
        sc = sc / score_div
        masked = jnp.where(lane < passages, sc, low)
        top = jnp.max(masked, axis=1, keepdims=True)
        lse = top + jnp.log(
            jnp.sum(jnp.where(lane < passages, jnp.exp(masked - top), 0.0), axis=1, keepdims=True)
        )
        hot = picked_ref[k]
        losses[k] = lse - jnp.sum(jnp.where(lane < passages, sc, 0.0) * hot, axis=1, keepdims=True) + jnp.zeros_like(sc)
        dscores[k] = jnp.where(
            valid, (jnp.exp(masked - lse) - hot) * (loss_scale / (G * q_count)), 0.0
        )
    loss_ref[...] = losses[g]

    mine = dscores[g]
    dq = jnp.zeros((8, C), jnp.float32)
    for p in range(passages):
        row = q_count + p % p_count
        dq = dq + mine[:, p : p + 1] * pooled[p // p_count, row : row + 1, :]

    def factor(row, dpool):
        sm = smooth[row]
        gate = jnp.where(sm > 0, 1.0 / (1.0 + jnp.maximum(sm, 0.0)), 0.0)
        coef[row] = dpool * (1.0 / score_div) * gate / total[row]

    for k in range(q_count):
        factor(k, dq[k : k + 1, :])
    for k in range(p_count):
        dp = jnp.zeros((8, C), jnp.float32)
        for group in range(G):
            column = jnp.sum(
                jnp.where(lane == g * p_count + k, dscores[group], 0.0), axis=1, keepdims=True
            )
            dp = dp + column * pooled[group]
        factor(q_count + k, jnp.sum(dp, axis=0, keepdims=True))

    for b in range(B):
        if b == 0:
            seqs = [(k, k * q_len, q_len) for k in range(q_count)]
        else:
            seqs = [(q_count + b - 1, 0, R)]
        for row, first, length in seqs:
            def body(n, carry, b=b, row=row, first=first, length=length):
                cols = pl.ds(pl.multiple_of(n * ptile, ptile), ptile)
                dl[pl.ds(b * R + first, length), cols] = (
                    acc[b, pl.ds(first, length), cols] * coef[row, :, cols]
                ).astype(jnp.bfloat16)
                return carry

            lax.fori_loop(0, C // ptile, body, 0)

    ftile = min(256, F)

    everything = pl.ds(0, B * R)

    def mm2(v, store, tokens=everything):
        def body(n, carry):
            at = pl.multiple_of(n * ftile, ftile)
            rows = pl.ds(pl.multiple_of(v * F + at, ftile), ftile)
            store(pl.ds(at, ftile), nt_dot(dl[tokens, :], w[rows, :]))
            return carry

        lax.fori_loop(0, F // ftile, body, 0)

    def sib_copy(b, j):
        rows = pl.ds(b * R if isinstance(b, int) else pl.multiple_of(b * R, R), R)
        return pltpu.make_async_remote_copy(
            src_ref=sib_out.at[j, rows], dst_ref=sib_in.at[j, rows],
            send_sem=send_sib.at[b, j], recv_sem=recv_sib.at[b, j],
            device_id={"vocab": sib}, device_id_type=MESH,
        )

    def right_copy(b, d):
        return pltpu.make_async_remote_copy(
            src_ref=out_r.at[b, d], dst_ref=in_l.at[b, d],
            send_sem=send_r.at[b, d], recv_sem=recv_l.at[b, d],
            device_id={"vocab": me + 2}, device_id_type=MESH,
        )

    def left_copy(b, d):
        return pltpu.make_async_remote_copy(
            src_ref=out_l.at[b, d], dst_ref=in_r.at[b, d],
            send_sem=send_l.at[b, d], recv_sem=recv_r.at[b, d],
            device_id={"vocab": me - 2}, device_id_type=MESH,
        )

    def for_sibling(j):
        def store(cols, value):
            sib_out[j, :, cols] = value.astype(jnp.bfloat16)

        mm2(2 * j + 1 - c, store)
        for b in range(B):
            sib_copy(b, j).start()

    def for_me(j, way):
        def store(cols, value):
            part[way, :, cols] = value

        mm2(2 * j + c, store)

    def pass_on(way, j, b, d, more, copy, arrived, out):
        rows = pl.ds(b * R, R)
        sib_copy(b, j).wait_recv()

        @pl.when(more)
        def _():
            copy(b, d).wait_recv()
            out[b, d - 1] = (
                part[way, rows]
                + sib_in[j, rows].astype(jnp.float32)
                + arrived[b, d].astype(jnp.float32)
            ).astype(jnp.bfloat16)

        @pl.when(jnp.logical_not(more))
        def _():
            out[b, d - 1] = (
                part[way, rows] + sib_in[j, rows].astype(jnp.float32)
            ).astype(jnp.bfloat16)

        copy(b, d - 1).start()

    def scatter_step(s, carry):
        d = L - 1 - s
        right, left = i + d, i - d
        go_right = right < L
        go_left = jnp.logical_and(left >= 0, d > 0)
        on_right = jnp.logical_and(go_right, d > 0)

        @pl.when(go_right)
        def _():
            for_sibling(right)

        @pl.when(go_left)
        def _():
            for_sibling(left)

        @pl.when(go_right)
        def _():
            for_me(right, 0)

        @pl.when(go_left)
        def _():
            for_me(left, 1)

        for b in range(B):
            @pl.when(on_right)
            def _(b=b):
                pass_on(0, right, b, d, has_left, right_copy, in_l, out_r)

            @pl.when(go_left)
            def _(b=b):
                pass_on(1, left, b, d, has_right, left_copy, in_r, out_l)

        return carry

    @pl.when(jnp.logical_or(i == 0, i == L - 1))
    def _():
        j = L - 1 - i

        def first(b, carry):
            rows = pl.ds(pl.multiple_of(b * R, R), R)

            def store_sib(cols, value):
                sib_out[j, rows, cols] = value.astype(jnp.bfloat16)

            def store_own(cols, value):
                part[0, rows, cols] = value

            mm2(2 * j + 1 - c, store_sib, rows)
            sib_copy(b, j).start()
            mm2(2 * j + c, store_own, rows)
            sib_copy(b, j).wait_recv()
            value = (part[0, rows] + sib_in[j, rows].astype(jnp.float32)).astype(jnp.bfloat16)

            @pl.when(i == 0)
            def _():
                out_r[b, L - 2] = value
                right_copy(b, L - 2).start()

            @pl.when(i == L - 1)
            def _():
                out_l[b, L - 2] = value
                left_copy(b, L - 2).start()

            return carry

        lax.fori_loop(0, B, first, 0)

    lax.fori_loop(1, L, scatter_step, 0)

    for b in range(B):
        rows = pl.ds(b * R, R)
        sib_copy(b, i).wait_recv()

        @pl.when(jnp.logical_and(has_left, has_right))
        def _():
            right_copy(b, 0).wait_recv()
            left_copy(b, 0).wait_recv()
            out_ref[rows, :] = (
                part[0, rows]
                + sib_in[i, rows].astype(jnp.float32)
                + in_l[b, 0].astype(jnp.float32)
                + in_r[b, 0].astype(jnp.float32)
            ).astype(jnp.bfloat16)

        @pl.when(jnp.logical_and(has_left, jnp.logical_not(has_right)))
        def _():
            right_copy(b, 0).wait_recv()
            out_ref[rows, :] = (
                part[0, rows]
                + sib_in[i, rows].astype(jnp.float32)
                + in_l[b, 0].astype(jnp.float32)
            ).astype(jnp.bfloat16)

        @pl.when(jnp.logical_and(jnp.logical_not(has_left), has_right))
        def _():
            left_copy(b, 0).wait_recv()
            out_ref[rows, :] = (
                part[0, rows]
                + sib_in[i, rows].astype(jnp.float32)
                + in_r[b, 0].astype(jnp.float32)
            ).astype(jnp.bfloat16)

        @pl.when(jnp.logical_not(jnp.logical_or(has_left, has_right)))
        def _():
            out_ref[rows, :] = (
                part[0, rows] + sib_in[i, rows].astype(jnp.float32)
            ).astype(jnp.bfloat16)

    for k in range(1, G):
        pooled_copy(g, k).wait_send()
    for k in range(1, V):
        score_copy(me, k).wait_send()

    def drain(s, carry):
        b, j = lax.div(s, L), lax.rem(s, L)
        v = 2 * j + c
        hop(v, b, 2, sib).wait_send()
        sib_copy(b, j).wait_send()

        @pl.when(jnp.logical_and(has_right, j <= i))
        def _():
            hop(v, b, 0, me + 2).wait_send()

        @pl.when(jnp.logical_and(has_left, j >= i))
        def _():
            hop(v, b, 1, me - 2).wait_send()

        @pl.when(jnp.logical_and(j > 0, i + j < L))
        def _():
            right_copy(b, j - 1).wait_send()

        @pl.when(jnp.logical_and(j > 0, i - j >= 0))
        def _():
            left_copy(b, j - 1).wait_send()

        return carry

    lax.fori_loop(0, B * L, drain, 0)


def on_device(G, V, query_hidden, passage_hidden, head_weight, query_mask, passage_mask, positive):
    q_count, q_len, F = query_hidden.shape
    p_count, p_len, _ = passage_hidden.shape
    D, C = head_weight.shape
    R = p_len
    assert q_count * q_len == R and q_count + p_count <= 8
    B = 1 + p_count
    L = V // 2
    hot = positive[:, None] == jnp.arange(lanes, dtype=jnp.int32)[None, :]
    picked = jnp.pad(
        hot.astype(jnp.float32).reshape(G, q_count, lanes), ((0, 0), (0, 8 - q_count), (0, 0))
    )
    cfg = (G, V, B, R, F, C, q_count, p_count, q_len)
    seqs = q_count + p_count
    bf, f32, dma = jnp.bfloat16, jnp.float32, pltpu.SemaphoreType.DMA
    vmem, anywhere = pl.BlockSpec(memory_space=pltpu.VMEM), pl.BlockSpec(memory_space=pl.ANY)
    line = pltpu.VMEM((B, L - 1, R, F), bf)
    grads, loss = pl.pallas_call(
        functools.partial(kernel, cfg),
        out_shape=(
            jax.ShapeDtypeStruct((B * R, F), bf),
            jax.ShapeDtypeStruct((8, lanes), f32),
        ),
        in_specs=[anywhere, anywhere, anywhere, vmem, vmem, vmem],
        out_specs=(vmem, vmem),
        scratch_shapes=[
            pltpu.VMEM((D, C), bf),
            pltpu.VMEM((V, B, R, F), bf),
            pltpu.VMEM((B, R, C), f32),
            pltpu.VMEM((B * R, C), bf),
            line, line, line, line,
            pltpu.VMEM((L, B * R, F), bf),
            pltpu.VMEM((L, B * R, F), bf),
            pltpu.VMEM((2, B * R, F), f32),
            pltpu.VMEM((seqs, 1, C), f32),
            pltpu.VMEM((seqs, 1, C), f32),
            pltpu.VMEM((seqs, 1, C), f32),
            pltpu.VMEM((G, 8, C), f32),
            pltpu.VMEM((V, G, 8, lanes), f32),
            pltpu.VMEM((G, 8, lanes), f32),
            pltpu.VMEM((G, 8, lanes), f32),
            dma((B,)),
            dma,
            dma((V, B)),
            dma((3, V, B)),
            dma((G,)),
            dma((G,)),
            dma((V,)),
            dma((V,)),
            dma((B, L - 1)),
            dma((B, L - 1)),
            dma((B, L - 1)),
            dma((B, L - 1)),
            dma((B, L)),
            dma((B, L)),
        ],
        compiler_params=pltpu.CompilerParams(
            collective_id=0, has_side_effects=True, vmem_limit_bytes=56 * 1024 * 1024
        ),
    )(
        query_hidden.reshape(R, F),
        passage_hidden.reshape(p_count * R, F),
        head_weight,
        query_mask,
        passage_mask,
        picked,
    )
    return (
        grads[:R].reshape(query_hidden.shape),
        grads[R:].reshape(passage_hidden.shape),
        loss[:q_count, 0],
    )


def solution(mesh):
    return jax.shard_map(
        functools.partial(on_device, mesh.shape["dp"], mesh.shape["vocab"]),
        mesh=mesh,
        in_specs=(
            P("dp", None, "vocab"),
            P("dp", None, "vocab"),
            P(None, "vocab"),
            P("dp", None),
            P("dp", None),
            P(),
        ),
        out_specs=(P("dp", None, "vocab"), P("dp", None, "vocab"), P("dp")),
        check_vma=False,
    )
```
